32 devices in a mesh: seq: 8 (over z, y), mp: 4 (over x, core).
Axes of the slice: x: 2, y: 2, z: 4, core: 2. Of those that a mesh axis runs over, the one named last changes fastest.
Arguments:
- q_branch: bfloat16 [16, 128, 2048], P('seq', None, 'mp'), may hold values from -4.5 to 4.5
- k_branch: bfloat16 [16, 128, 2048], P('seq', None, 'mp'), may hold values from -6 to 6
- v_branch: bfloat16 [16, 128, 2048], P('seq', None, 'mp'), may hold values from -6 to 6
- d_out: bfloat16 [16, 128, 2048], P('seq', 'mp'), may hold values from -24 to 24
- k_prefix: bfloat16 [768, 1, 2048], P('seq', None, 'mp'), may hold values from -4.5 to 4.5
- v_prefix: bfloat16 [768, 1, 2048], P('seq', None, 'mp'), may hold values from -6 to 6
- slot_branch: int32 [16], replicated, may hold values from 0 to 15, each once
- branch_len: int32 [16], replicated, may hold values from 1 to 128, 1280 in all
Outputs:
- query_grad: bfloat16 [16, 128, 2048], P('seq', None, 'mp')
- branch_key_grad: bfloat16 [16, 128, 2048], P('seq', None, 'mp')
- branch_value_grad: bfloat16 [16, 128, 2048], P('seq', None, 'mp')
- prefix_key_grad: bfloat16 [768, 1, 2048], P('seq', None, 'mp')
- prefix_value_grad: bfloat16 [768, 1, 2048], P('seq', None, 'mp')
The draws below stay inside these ranges and needn't reach their ends.
Inputs may be any that keep to these rules, and one draw needn't show every extreme that they name: `slot_branch`: each branch stands in exactly one slot. `branch_len`: some branch has exactly 128 frames.
All inputs are finite; a program needn't handle non-finite values.
Results may differ from the reference program's by a relative error of at most 0.0084.
Values may be sent and summed in bfloat16 or wider, within the bound.
A program may use at most 128 MiB of HBM per device.

```python
import math
import jax
import jax.numpy as jnp
import numpy as np
from jax import lax

HEADS = 16
HEAD = 128
NPRE = 1
BLEN = 128
PREFIX = 768
BRANCHES = 16


def draw_k_prefix(key, part):
    key = jax.random.fold_in(key, 3)
    full_shape = (PREFIX, NPRE, HEADS, HEAD)
    base_draw = jnp.clip(jax.random.normal(key, full_shape, jnp.float32), -4.5, 4.5)
    return base_draw.reshape(PREFIX, NPRE, HEADS * HEAD).astype(jnp.bfloat16)


def draw_q_branch(key, part):
    key = jax.random.fold_in(key, 5)
    full_shape = (BRANCHES, BLEN, HEADS, HEAD)
    base_draw = jnp.clip(jax.random.normal(key, full_shape, jnp.float32), -4.5, 4.5)
    return base_draw.reshape(BRANCHES, BLEN, HEADS * HEAD).astype(jnp.bfloat16)


def level_of(key, shape, pieces, smallest, high):
    def one(axis_at, parts):
        heights = jax.random.uniform(jax.random.fold_in(jax.random.fold_in(key, 6), axis_at), (parts,), jnp.float32, smallest / len(pieces), high / len(pieces))
        return jnp.repeat(jnp.exp(heights), shape[axis_at] // parts).reshape((-1,) + (1,) * (len(shape) - axis_at - 1))

    level = one(*pieces[0])
    for cut in pieces[1:]:
        level = level * one(*cut)
    return level


def split_up(number_of, total, reach, skew):
    weights = [(1 << 20) // math.isqrt(grade ** skew) + 1 for grade in range(2, number_of + 1)]
    surplus, holding = total - reach - (number_of - 1), [1] * (number_of - 1)
    while surplus > 0:
        free = [i for i in range(number_of - 1) if holding[i] < reach]
        mass, budget = sum([weights[i] for i in free]), surplus
        for i in free:
            extra = min(reach - holding[i], max(1, budget * weights[i] // mass), surplus)
            holding[i] = holding[i] + extra
            surplus = surplus - extra
    return np.array([reach] + holding)


def ragged_sizes(own_key, count, total, reach, skew):
    if count == 2:
        one = jax.random.randint(own_key, (), max(1, total - reach), min(reach, total - 1) + 1)
        return jnp.stack([one, total - one])
    tallies = jnp.asarray(split_up(count, total, reach, skew), jnp.int32)
    couples = (count - 1) // 2
    donor, taker = tallies[1:1 + 2 * couples:2], tallies[2:2 + 2 * couples:2]
    room = jnp.minimum(donor - 1, reach - taker)
    shifted = jax.random.randint(jax.random.fold_in(own_key, 1), (couples,), 0, 1 << 20) % (room + 1)
    tallies = tallies.at[1:1 + 2 * couples:2].set(donor - shifted).at[2:2 + 2 * couples:2].set(taker + shifted)
    return tallies[jax.random.permutation(jax.random.fold_in(own_key, 2), count)]


def noise(key, shape, deviation, reach, cuts=(), kind=jnp.bfloat16):
    result = deviation * jax.random.normal(key, shape, jnp.float32)
    if cuts:
        result = result * level_of(key, shape, cuts, -0.22, 0.18)
    return jnp.clip(result, -reach, reach).astype(kind)


def setup_inputs(seed: int = 0) -> dict:
    splits = jax.random.split(jax.random.key(seed), 9)
    q_branch = draw_q_branch(jax.random.fold_in(splits[8], 71), 0)
    k_branch = noise(splits[1], (BRANCHES, BLEN, HEADS * HEAD), 1.0, 6.0, ((0, 8), (2, 4)))
    v_branch = noise(splits[2], (BRANCHES, BLEN, HEADS * HEAD), 1.0, 6.0, ((0, 8), (2, 4)))
    d_out = noise(splits[3], (BRANCHES, BLEN, HEADS * HEAD), 4.0, 24.0, ((0, 8), (1, 4)))
    k_prefix = draw_k_prefix(jax.random.fold_in(splits[8], 71), 0)
    v_prefix = noise(splits[5], (PREFIX, NPRE, HEADS * HEAD), 1.0, 6.0, ((0, 8), (2, 4)))
    slot_branch = jax.random.permutation(splits[6], BRANCHES).astype(jnp.int32)
    branch_len = ragged_sizes(splits[7], BRANCHES, BRANCHES * BLEN * 5 // 8, BLEN, 2).astype(jnp.int32)
    return {"q_branch": q_branch, "k_branch": k_branch, "v_branch": v_branch, "d_out": d_out, "k_prefix": k_prefix, "v_prefix": v_prefix, "slot_branch": slot_branch, "branch_len": branch_len}


def slot_grads(query_rows, key_rows, value_rows, cotangent_rows, chosen_keys, chosen_values, length):
    score_scale = 1.0 / math.sqrt(HEAD)
    key_block = jnp.concatenate([chosen_keys, key_rows], 0).astype(jnp.float32)
    value_block = jnp.concatenate([chosen_values, value_rows], 0).astype(jnp.float32)
    query_block = query_rows.astype(jnp.float32)
    scores = jnp.einsum('ihe,jhe->hij', query_block, key_block) * score_scale
    query_pos = jnp.arange(BLEN, dtype=jnp.int32)[:, None]
    key_pos = jnp.arange(PREFIX + BLEN, dtype=jnp.int32)[None, :] - PREFIX
    scores = jnp.where((key_pos <= query_pos)[None], scores, -jnp.inf)
    row_max = lax.optimization_barrier(jnp.max(scores, -1, keepdims=True))
    log_total = row_max + jnp.log(lax.optimization_barrier(jnp.sum(jnp.exp(scores - row_max), -1, keepdims=True)))
    exact_probs = jnp.exp(scores - log_total)
    weights = lax.optimization_barrier(exact_probs.astype(jnp.bfloat16)).astype(jnp.float32)
    attended = jnp.einsum('hij,jhe->ihe', weights, value_block)
    live_rows = jnp.arange(BLEN, dtype=jnp.int32) < length
    masked = jnp.where(live_rows[:, None, None], cotangent_rows, jnp.zeros_like(cotangent_rows)).astype(jnp.float32)
    row_delta = lax.optimization_barrier(jnp.sum(masked * attended, -1))
    grad_prob = jnp.einsum('ihe,jhe->hij', masked, value_block)
    grad_score = exact_probs * (grad_prob - jnp.transpose(row_delta)[:, :, None])
    grad_score = lax.optimization_barrier(grad_score.astype(jnp.bfloat16)).astype(jnp.float32)
    grad_q = jnp.einsum('hij,jhe->ihe', grad_score, key_block) * score_scale
    grad_k = jnp.einsum('hij,ihe->jhe', grad_score, query_block) * score_scale
    grad_v = jnp.einsum('hij,ihe->jhe', weights, masked)
    return (grad_q, grad_k, grad_v)

def reference(q_branch, k_branch, v_branch, d_out, k_prefix, v_prefix, slot_branch, branch_len):
    full_shape = (BRANCHES, BLEN, HEADS, HEAD)
    queries = q_branch.reshape(full_shape)
    branch_keys = k_branch.reshape(full_shape)
    branch_values = v_branch.reshape(full_shape)
    cotangents = d_out.reshape(full_shape)
    prefix_shape = (PREFIX, NPRE, HEADS, HEAD)
    all_keys = k_prefix.reshape(prefix_shape)
    all_values = v_prefix.reshape(prefix_shape)
    chosen_keys = all_keys[:, 0]
    chosen_values = all_values[:, 0]

    def one_slot(totals, slot_index):
        total_k, total_v = totals
        branch = slot_branch[slot_index]
        length = branch_len[branch]
        grad_q, grad_k, grad_v = slot_grads(queries[slot_index], branch_keys[slot_index], branch_values[slot_index], cotangents[slot_index], chosen_keys, chosen_values, length)
        total_k = total_k + grad_k[:PREFIX][:, None]
        total_v = total_v + grad_v[:PREFIX][:, None]
        outputs = (grad_q.astype(jnp.bfloat16), grad_k[PREFIX:].astype(jnp.bfloat16), grad_v[PREFIX:].astype(jnp.bfloat16))
        return ((total_k, total_v), outputs)
    zero_terms = jnp.zeros(prefix_shape, jnp.float32)
    (total_k, total_v), (grad_q, grad_k, grad_v) = lax.scan(one_slot, (zero_terms, zero_terms), jnp.arange(BRANCHES, dtype=jnp.int32))
    flat = (BRANCHES, BLEN, HEADS * HEAD)
    prefix_flat = (PREFIX, NPRE, HEADS * HEAD)
    return (grad_q.reshape(flat), grad_k.reshape(flat), grad_v.reshape(flat), total_k.astype(jnp.bfloat16).reshape(prefix_flat), total_v.astype(jnp.bfloat16).reshape(prefix_flat))
```

```python
import functools
import math

import jax
import jax.numpy as jnp
from jax import lax
from jax.experimental import pallas as pl
from jax.experimental.pallas import tpu as pltpu
from jax.sharding import PartitionSpec as P

HEAD = 128
MESH = pl.DeviceIdType.MESH
F32 = jnp.float32
BF16 = jnp.bfloat16
VMEM_LIMIT = 56 * 1024 * 1024


def dot_nt(a, b):
    return lax.dot_general(a, b, (((1,), (1,)), ((), ())), preferred_element_type=F32)


def dot_nn(a, b):
    return lax.dot_general(a, b, (((1,), (0,)), ((), ())), preferred_element_type=F32)


def dot_tn(a, b):
    return lax.dot_general(a, b, (((0,), (0,)), ((), ())), preferred_element_type=F32)


def fused_kernel(
    nseq,
    nmp,
    slots_ref,
    lens_ref,
    q_in,
    k_in,
    v_in,
    do_ref,
    kp_ref,
    vp_ref,
    dq_out,
    dbk_out,
    dbv_out,
    dpk_ref,
    dpv_ref,
    kv,
    dob,
    dom,
    st,
    dp,
    sb,
    db,
    mx,
    wt,
    ds,
    wb,
    dsb,
    part,
    ysend,
    yrecv,
    zsend,
    zrecv,
    q_ref,
    k_ref,
    v_ref,
    dq_ref,
    dbk_ref,
    dbv_ref,
    a_send,
    a_recv,
    d_send,
    d_recv,
    y_send,
    y_recv,
    z_send,
    z_recv,
    own_sem,
):
    slots, frames, cols = q_in.shape
    heads = cols // HEAD
    queries = slots * frames
    rows = kp_ref.shape[0]
    nz = nseq // 2
    scale = 1.0 / math.sqrt(HEAD)
    me = lax.axis_index("seq")
    m = lax.axis_index("mp")
    z = me // 2
    y = lax.rem(me, 2)
    oy = 1 - y
    up, down, across = me + 2, me - 2, z * 2 + oy
    has_up = z < nz - 1
    has_down = z > 0

    def chunk(zz, yy):
        return zz * 2 + yy

    pairs = ((q_in, q_ref), (k_in, k_ref), (v_in, v_ref))
    loads = [pltpu.make_async_copy(a, b, own_sem.at[i]) for i, (a, b) in enumerate(pairs)]
    pairs = ((dq_ref, dq_out), (dbk_ref, dbk_out), (dbv_ref, dbv_out))
    stores = [pltpu.make_async_copy(a, b, own_sem.at[3 + i]) for i, (a, b) in enumerate(pairs)]

    barrier = pltpu.get_barrier_semaphore()

    def greet(seq_index, mp_index):
        pl.semaphore_signal(barrier, inc=1, device_id=(seq_index, mp_index), device_id_type=MESH)

    for step in range(1, nmp):
        greet(me, lax.rem(m + step, nmp))
    greet(across, m)

    @pl.when(has_up)
    def _():
        greet(up, m)

    @pl.when(has_down)
    def _():
        greet(down, m)

    for load in loads:
        load.start()
    kv[0, me] = kp_ref[...]
    kv[1, me] = vp_ref[...]
    peers = nmp + jnp.where(has_up, 1, 0) + jnp.where(has_down, 1, 0)
    pl.semaphore_wait(barrier, peers)

    def ag_copy(side, which, zz, yy, target):
        c = chunk(zz, yy)
        return pltpu.make_async_remote_copy(
            src_ref=kv.at[which, c],
            dst_ref=kv.at[which, c],
            send_sem=a_send.at[side, which, zz],
            recv_sem=a_recv.at[which, c],
            device_id=(target, m),
            device_id_type=MESH,
        )

    def do_copy(sender, target, src_block):
        return pltpu.make_async_remote_copy(
            src_ref=do_ref.at[:, :, pl.ds(pl.multiple_of(src_block * cols, 128), cols)],
            dst_ref=dob.at[sender],
            send_sem=d_send.at[target],
            recv_sem=d_recv.at[sender],
            device_id=(me, target),
            device_id_type=MESH,
        )

    for which in range(2):

        @pl.when(has_up)
        def _():
            ag_copy(0, which, z, y, up).start()

        @pl.when(has_down)
        def _():
            ag_copy(1, which, z, y, down).start()

        ag_copy(2, which, z, y, across).start()
    for step in range(1, nmp):
        target = lax.rem(m + step, nmp)
        do_copy(m, target, target).start()
    dob[m] = do_ref[:, :, pl.ds(pl.multiple_of(m * cols, 128), cols)]

    def head_cols(h):
        return slice(h * HEAD, (h + 1) * HEAD)

    def q_head(h):
        return q_ref[:, :, head_cols(h)].reshape(queries, HEAD)

    def fold_max(x):
        return jnp.max(x.reshape(x.shape[0] // 8, 8, x.shape[1]), axis=0)

    def fold_sum(x):
        return jnp.sum(x.reshape(x.shape[0] // 8, 8, x.shape[1]), axis=0)

    for load in loads:
        load.wait()
    key_pos = lax.broadcasted_iota(jnp.int32, (frames, frames), 0)
    query_pos = lax.broadcasted_iota(jnp.int32, (frames, frames), 1)
    seen = key_pos <= query_pos
    for h in range(heads):
        for s in range(slots):
            scores = dot_nt(k_ref[s, :, head_cols(h)], q_ref[s, :, head_cols(h)])
            scores = jnp.where(seen, scores, -jnp.inf)
            sb[h, :, s * frames : (s + 1) * frames] = scores
            mx[h, :, s * frames : (s + 1) * frames] = fold_max(scores)

    for step in range(1, nmp):
        sender = lax.rem(m + nmp - step, nmp)
        do_copy(sender, sender, m).wait_recv()
    row_at = lax.broadcasted_iota(jnp.int32, (frames, cols), 0)
    for s in range(slots):
        length = lens_ref[slots_ref[me * slots + s]]
        rows_in = dob[:, s].reshape(frames, cols)
        dom[s * frames : (s + 1) * frames, :] = jnp.where(
            row_at < length, rows_in, jnp.zeros_like(rows_in)
        )
    for h in range(heads):
        for s in range(slots):
            db[h, :, s * frames : (s + 1) * frames] = dot_nt(
                v_ref[s, :, head_cols(h)], dom[s * frames : (s + 1) * frames, head_cols(h)]
            )

    def take_chunk(c):
        for h in range(heads):
            scores = dot_nt(kv[0, c, :, head_cols(h)], q_head(h))
            st[h, c] = scores
            mx[h] = jnp.maximum(mx[h], fold_max(scores))
            dp[h, c] = dot_nt(kv[1, c, :, head_cols(h)], dom[:, head_cols(h)])

    def wait_z(zz):
        for which in range(2):
            ag_copy(2, which, zz, y, across).wait_recv()

    def take_across(zz):
        for which in range(2):
            ag_copy(2, which, zz, oy, across).wait_recv()
        take_chunk(chunk(zz, oy))

    take_chunk(me)
    for t in range(1, nz):
        below, above = z - t, z + t

        @pl.when(below >= 0)
        def _():
            for which in range(2):
                ag_copy(0, which, below, y, across).wait_recv()

                @pl.when(has_up)
                def _():
                    ag_copy(0, which, below, y, up).start()

                ag_copy(2, which, below, y, across).start()

        @pl.when(above < nz)
        def _():
            for which in range(2):
                ag_copy(1, which, above, y, across).wait_recv()

                @pl.when(has_down)
                def _():
                    ag_copy(1, which, above, y, down).start()

                ag_copy(2, which, above, y, across).start()

        @pl.when(below >= 0)
        def _():
            take_chunk(chunk(below, y))

        @pl.when(above < nz)
        def _():
            take_chunk(chunk(above, y))

        if t == 1:
            take_across(z)
        else:

            @pl.when(z - (t - 1) >= 0)
            def _():
                take_across(z - (t - 1))

            @pl.when(z + (t - 1) < nz)
            def _():
                take_across(z + (t - 1))

    @pl.when(z - (nz - 1) >= 0)
    def _():
        take_across(z - (nz - 1))

    @pl.when(z + (nz - 1) < nz)
    def _():
        take_across(z + (nz - 1))

    for h in range(heads):
        top = jnp.max(mx[h], axis=0, keepdims=True)
        total = jnp.zeros((8, queries), F32)
        delta = jnp.zeros((8, queries), F32)
        for c in range(nseq):
            e = jnp.exp((st[h, c] - top) * scale)
            st[h, c] = e
            total = total + fold_sum(e)
            delta = delta + fold_sum(e * dp[h, c])
        e = jnp.exp((sb[h] - top) * scale)
        sb[h] = e
        total = total + fold_sum(e)
        delta = delta + fold_sum(e * db[h])
        inverse = 1.0 / jnp.sum(total, axis=0, keepdims=True)
        delta = jnp.sum(delta, axis=0, keepdims=True) * inverse
        for c in range(nseq):
            p = st[h, c] * inverse
            wt[h, c] = p.astype(BF16)
            ds[h, c] = (p * (dp[h, c] - delta)).astype(BF16)
        p = sb[h] * inverse
        wb[h] = p.astype(BF16)
        dsb[h] = (p * (db[h] - delta)).astype(BF16)

    def y_copy(which, zz):
        return pltpu.make_async_remote_copy(
            src_ref=ysend.at[which, zz],
            dst_ref=yrecv.at[which, zz],
            send_sem=y_send.at[which, zz],
            recv_sem=y_recv.at[which, zz],
            device_id=(across, m),
            device_id_type=MESH,
        )

    order = []
    low, high = 0, nz - 1
    for _ in range(nz):
        take_high = high - z >= z - low
        order.append(jnp.where(take_high, high, low))
        low, high = jnp.where(take_high, low, low + 1), jnp.where(take_high, high - 1, high)
    for zz in order:
        c = chunk(zz, oy)
        for h in range(heads):
            ysend[0, zz, :, head_cols(h)] = (dot_nn(ds[h, c], q_head(h)) * scale).astype(BF16)
        y_copy(0, zz).start()
        for h in range(heads):
            ysend[1, zz, :, head_cols(h)] = dot_nn(wt[h, c], dom[:, head_cols(h)]).astype(BF16)
        y_copy(1, zz).start()
    for zz in order:
        c = chunk(zz, y)
        for h in range(heads):
            part[0, zz, :, head_cols(h)] = dot_nn(ds[h, c], q_head(h)) * scale
            part[1, zz, :, head_cols(h)] = dot_nn(wt[h, c], dom[:, head_cols(h)])

    def z_copy(side, which, zz, target):
        return pltpu.make_async_remote_copy(
            src_ref=zsend.at[side, which, zz],
            dst_ref=zrecv.at[side, which, zz],
            send_sem=z_send.at[side, which, zz],
            recv_sem=z_recv.at[side, which, zz],
            device_id=(target, m),
            device_id_type=MESH,
        )

    def relay(side, zz, has_source, target):
        for which in range(2):
            y_copy(which, zz).wait_recv()
            part[which, zz] = part[which, zz] + yrecv[which, zz].astype(F32)

            @pl.when(has_source)
            def _():
                z_copy(side, which, zz, target).wait_recv()
                part[which, zz] = part[which, zz] + zrecv[side, which, zz].astype(F32)

            zsend[side, which, zz] = part[which, zz].astype(BF16)
            z_copy(side, which, zz, target).start()

    def query_grads(h):
        keys = kv[0, :, :, head_cols(h)].reshape(nseq * rows, HEAD)
        grad = dot_tn(ds[h].reshape(nseq * rows, queries), keys)
        for s in range(slots):
            at = slice(s * frames, (s + 1) * frames)
            own = dot_tn(dsb[h, :, at], k_ref[s, :, head_cols(h)])
            dq_ref[s, :, head_cols(h)] = ((grad[at] + own) * scale).astype(BF16)
            dbk_ref[s, :, head_cols(h)] = (
                dot_nn(dsb[h, :, at], q_ref[s, :, head_cols(h)]) * scale
            ).astype(BF16)
            dbv_ref[s, :, head_cols(h)] = dot_nn(wb[h, :, at], dom[at, head_cols(h)]).astype(BF16)

    for h in range(heads):
        query_grads(h)
    for store in stores:
        store.start()
    for zz in order[:-1]:

        @pl.when(zz > z)
        def _():
            relay(0, zz, has_down, up)

        @pl.when(zz < z)
        def _():
            relay(1, zz, has_up, down)

    for which, out in ((0, dpk_ref), (1, dpv_ref)):
        y_copy(which, z).wait_recv()
        part[which, z] = part[which, z] + yrecv[which, z].astype(F32)

        @pl.when(has_down)
        def _():
            z_copy(0, which, z, across).wait_recv()
            part[which, z] = part[which, z] + zrecv[0, which, z].astype(F32)

        @pl.when(has_up)
        def _():
            z_copy(1, which, z, across).wait_recv()
            part[which, z] = part[which, z] + zrecv[1, which, z].astype(F32)

        out[...] = part[which, z].astype(BF16)

    for store in stores:
        store.wait()
    for step in range(1, nmp):
        target = lax.rem(m + step, nmp)
        do_copy(m, target, target).wait_send()
    for zz in range(nz):
        for which in range(2):
            ag_copy(2, which, zz, y, across).wait_send()
            y_copy(which, zz).wait_send()

            @pl.when(jnp.logical_and(has_up, zz <= z))
            def _():
                ag_copy(0, which, zz, y, up).wait_send()

            @pl.when(jnp.logical_and(has_down, zz >= z))
            def _():
                ag_copy(1, which, zz, y, down).wait_send()

            @pl.when(z < zz)
            def _():
                z_copy(0, which, zz, up).wait_send()

            @pl.when(z > zz)
            def _():
                z_copy(1, which, zz, down).wait_send()


def hand_over(*refs):
    count = len(refs) // 2
    sems = refs[-1]
    copies = [
        pltpu.make_async_copy(refs[i], refs[count + i], sems.at[i]) for i in range(count)
    ]
    for copy in copies:
        copy.start()
    for copy in copies:
        copy.wait()


def scratch_list(nseq, nmp, slots, frames, cols, rows):
    heads, queries, nz = cols // HEAD, slots * frames, nseq // 2
    return [
        ((2, nseq, rows, cols), BF16),
        ((nmp, slots, frames // nmp, cols), BF16),
        ((queries, cols), BF16),
        ((heads, nseq, rows, queries), F32),
        ((heads, nseq, rows, queries), F32),
        ((heads, frames, queries), F32),
        ((heads, frames, queries), F32),
        ((heads, 8, queries), F32),
        ((heads, nseq, rows, queries), BF16),
        ((heads, nseq, rows, queries), BF16),
        ((heads, frames, queries), BF16),
        ((heads, frames, queries), BF16),
        ((2, nz, rows, cols), F32),
        ((2, nz, rows, cols), BF16),
        ((2, nz, rows, cols), BF16),
        ((2, 2, nz, rows, cols), BF16),
        ((2, 2, nz, rows, cols), BF16),
    ] + [((slots, frames, cols), BF16)] * 6


def fused_body(nseq, nmp, q_branch, k_branch, v_branch, d_out, k_prefix, v_prefix, slot_branch, branch_len):
    slots, frames, cols = q_branch.shape
    rows = k_prefix.shape[0]
    nz = nseq // 2
    scratch = [
        pltpu.VMEM(shape, dtype)
        for shape, dtype in scratch_list(nseq, nmp, slots, frames, cols, rows)
    ]
    dma = pltpu.SemaphoreType.DMA
    sems = [
        dma((3, 2, nz)),
        dma((2, nseq)),
        dma((nmp,)),
        dma((nmp,)),
        dma((2, nz)),
        dma((2, nz)),
        dma((2, 2, nz)),
        dma((2, 2, nz)),
        dma((6,)),
    ]
    vmem = pl.BlockSpec(memory_space=pltpu.VMEM)
    smem = pl.BlockSpec(memory_space=pltpu.SMEM)
    anywhere = pl.BlockSpec(memory_space=pl.ANY)
    branch = jax.ShapeDtypeStruct((slots, frames, cols), BF16)
    prefix = jax.ShapeDtypeStruct((rows, cols), BF16)
    dq, dbk, dbv, dpk, dpv = pl.pallas_call(
        functools.partial(fused_kernel, nseq, nmp),
        out_shape=(branch, branch, branch, prefix, prefix),
        in_specs=[smem] * 2 + [anywhere] * 3 + [vmem] * 3,
        out_specs=(anywhere,) * 3 + (vmem,) * 2,
        scratch_shapes=scratch + sems,
        compiler_params=pltpu.CompilerParams(
            collective_id=0, has_side_effects=True, vmem_limit_bytes=VMEM_LIMIT
        ),
        name="attention_backward",
    )(
        slot_branch,
        branch_len,
        q_branch,
        k_branch,
        v_branch,
        d_out,
        k_prefix[:, 0],
        v_prefix[:, 0],
    )
    dq, dbk, dbv, dpk, dpv = pl.pallas_call(
        hand_over,
        out_shape=(branch, branch, branch, prefix, prefix),
        in_specs=[vmem] * 5,
        out_specs=(anywhere,) * 5,
        scratch_shapes=[dma((5,))],
        name="hand_over",
    )(dq, dbk, dbv, dpk, dpv)
    return dq, dbk, dbv, dpk[:, None], dpv[:, None]


def fits(nseq, nmp, slots, frames, cols, rows):
    if nseq % 2 or rows % 16 or (frames // nmp) % 16 or cols % HEAD:
        return False
    held = sum(
        math.prod(shape) * jnp.dtype(dtype).itemsize
        for shape, dtype in scratch_list(nseq, nmp, slots, frames, cols, rows)
    )
    return held < VMEM_LIMIT // 2


def pick_prefix(gathered, slot_count):
    row_list = [gathered[:, 0] for slot_index in range(slot_count)]
    return jnp.stack(row_list, 0)


def by_prefix(grad_rows):
    summed = grad_rows[0]
    summed = summed + grad_rows[1]
    return summed[:, None, :]


def merge_heads(stacked):
    head_count, slot_count, frames, width = stacked.shape
    return jnp.transpose(stacked, (1, 2, 0, 3)).reshape(slot_count, frames, head_count * width)


def merge_prefix(stacked):
    head_count, prefix_rows, prefix_count, width = stacked.shape
    return jnp.transpose(stacked, (1, 2, 0, 3)).reshape(
        prefix_rows, prefix_count, head_count * width
    )


def plain_body(q_branch, k_branch, v_branch, d_out, k_prefix, v_prefix, slot_branch, branch_len):
    score_scale = 1.0 / math.sqrt(HEAD)
    slot_count = q_branch.shape[0]
    frames = q_branch.shape[1]
    local_heads = q_branch.shape[2] // HEAD
    own_branches = lax.dynamic_slice_in_dim(
        slot_branch, lax.axis_index("seq") * slot_count, slot_count
    )
    branch_hits = (
        own_branches[:, None] == jnp.arange(slot_branch.shape[0], dtype=jnp.int32)[None, :]
    )
    lengths = jnp.sum(jnp.where(branch_hits, branch_len[None, :], 0), 1)
    cotangent = lax.all_to_all(d_out, "mp", split_axis=2, concat_axis=1, tiled=True)
    live_rows = jnp.arange(frames, dtype=jnp.int32)[None, :, None] < lengths[:, None, None]
    masked = jnp.where(live_rows, cotangent, jnp.zeros_like(cotangent))
    prefix_keys, prefix_values = (
        lax.all_gather(k_prefix, "seq", axis=0, tiled=True),
        lax.all_gather(v_prefix, "seq", axis=0, tiled=True),
    )
    prefix_rows = prefix_keys.shape[0]
    key_pick = pick_prefix(prefix_keys, slot_count)
    value_pick = pick_prefix(prefix_values, slot_count)
    query_pos = jnp.arange(frames, dtype=jnp.int32)[:, None]
    key_pos = jnp.arange(prefix_rows + frames, dtype=jnp.int32)[None, :] - prefix_rows
    allowed = (key_pos <= query_pos)[None]

    def per_head(head_index):
        column_start = head_index * HEAD
        query_head = lax.dynamic_slice_in_dim(q_branch, column_start, HEAD, 2)
        cotangent_head = lax.dynamic_slice_in_dim(masked, column_start, HEAD, 2)
        key_block = jnp.concatenate(
            [
                lax.dynamic_slice_in_dim(key_pick, column_start, HEAD, 2),
                lax.dynamic_slice_in_dim(k_branch, column_start, HEAD, 2),
            ],
            1,
        )
        value_block = jnp.concatenate(
            [
                lax.dynamic_slice_in_dim(value_pick, column_start, HEAD, 2),
                lax.dynamic_slice_in_dim(v_branch, column_start, HEAD, 2),
            ],
            1,
        )
        scores = (
            jnp.einsum("sie,sje->sij", query_head, key_block, preferred_element_type=jnp.float32)
            * score_scale
        )
        scores = jnp.where(allowed, scores, -jnp.inf)
        row_max = jnp.max(scores, -1, keepdims=True)
        log_total = row_max + jnp.log(jnp.sum(jnp.exp(scores - row_max), -1, keepdims=True))
        exact_probs = jnp.exp(scores - log_total)
        weights = exact_probs.astype(jnp.bfloat16)
        attended = jnp.einsum(
            "sij,sje->sie", weights, value_block, preferred_element_type=jnp.float32
        )
        row_delta = jnp.sum(cotangent_head.astype(jnp.float32) * attended, -1, keepdims=True)
        grad_prob = jnp.einsum(
            "sie,sje->sij", cotangent_head, value_block, preferred_element_type=jnp.float32
        )
        grad_score = (exact_probs * (grad_prob - row_delta)).astype(jnp.bfloat16)
        grad_q = (
            jnp.einsum("sij,sje->sie", grad_score, key_block, preferred_element_type=jnp.float32)
            * score_scale
        ).astype(jnp.bfloat16)
        grad_k = (
            jnp.einsum("sij,sie->sje", grad_score, query_head, preferred_element_type=jnp.float32)
            * score_scale
        )
        grad_v = jnp.einsum(
            "sij,sie->sje", weights, cotangent_head, preferred_element_type=jnp.float32
        )
        branch_k = grad_k[:, prefix_rows:].astype(jnp.bfloat16)
        branch_v = grad_v[:, prefix_rows:].astype(jnp.bfloat16)
        return (
            grad_q,
            branch_k,
            branch_v,
            by_prefix(grad_k[:, :prefix_rows]),
            by_prefix(grad_v[:, :prefix_rows]),
        )

    head_results = lax.map(per_head, jnp.arange(local_heads, dtype=jnp.int32))
    query_grad = merge_heads(head_results[0])
    branch_key_grad = merge_heads(head_results[1])
    branch_value_grad = merge_heads(head_results[2])
    summed_k, summed_v = (
        lax.psum_scatter(merge_prefix(head_results[3]), "seq", scatter_dimension=0, tiled=True),
        lax.psum_scatter(merge_prefix(head_results[4]), "seq", scatter_dimension=0, tiled=True),
    )
    return (
        query_grad,
        branch_key_grad,
        branch_value_grad,
        summed_k.astype(jnp.bfloat16),
        summed_v.astype(jnp.bfloat16),
    )


def body(nseq, nmp, *arrays):
    slots, frames, cols = arrays[0].shape
    if fits(nseq, nmp, slots, frames, cols, arrays[4].shape[0]):
        return fused_body(nseq, nmp, *arrays)
    return plain_body(*arrays)


def solution(mesh):
    in_specs = (
        P("seq", None, "mp"),
        P("seq", None, "mp"),
        P("seq", None, "mp"),
        P("seq", "mp", None),
        P("seq", None, "mp"),
        P("seq", None, "mp"),
        P(),
        P(),
    )
    out_specs = (
        P("seq", None, "mp"),
        P("seq", None, "mp"),
        P("seq", None, "mp"),
        P("seq", None, "mp"),
        P("seq", None, "mp"),
    )
    return jax.shard_map(
        functools.partial(body, mesh.shape["seq"], mesh.shape["mp"]),
        mesh=mesh,
        in_specs=in_specs,
        out_specs=out_specs,
        check_vma=False,
    )
```
